512 devices in a mesh: ctx: 16 (over z_lo, y), basis: 32 (over z_hi, x, core).
Axes of the slice: x: 4, y: 8, z: 8 (z_hi: 4, z_lo: 2; z = z_hi * 2 + z_lo), core: 2. Of those that a mesh axis runs over, the one named last changes fastest.
Arguments:
- out_grad: bfloat16 [4608, 8192], P('ctx', 'basis'), may hold values from -6 to 6
- inputs: bfloat16 [4608, 8192], P('ctx', 'basis'), may hold values from -6 to 6
- basis_out: bfloat16 [8192, 4096], P(None, 'basis'), may hold values from -0.0625 to 0.0625
- basis_in: bfloat16 [8192, 4096], P(None, 'basis'), may hold values from -0.0625 to 0.0625
- correction: float32 [4096, 4096], P('basis', 'ctx'), may hold values from 0.5 to 2
Outputs:
- updated: float32 [4096, 4096], P('basis', 'ctx')
The draws below stay inside these ranges and needn't reach their ends.
All inputs are finite; a program needn't handle non-finite values.
Results may differ from the reference program's by a relative error of at most 0.0032.
Values may be sent and summed in bfloat16 or wider, within the bound.
A program may use at most 64 MiB of HBM per device.

```python
import jax
import jax.numpy as jnp

D = 8192
KG = 4096
KA = 4096
GROUPS = 2
TOK_DEV = 288
TOKENS = 4608
N_CTX = 16


def steps_of(own_key, extent, pieces, least, high):
    factor_of, own = 1.0, jax.random.fold_in(own_key, 6)
    for position, parts in pieces:
        steps = jnp.exp(jax.random.uniform(jax.random.fold_in(own, position), (parts,), jnp.float32, least / len(pieces), high / len(pieces)))
        factor_of = factor_of * jnp.repeat(steps, extent[position] // parts).reshape([-1 if axis == position else 1 for axis in range(len(extent))])
    return factor_of


def centred(rng, shape, deviation, reach, shards=(), dtype=jnp.bfloat16):
    loudness = steps_of(rng, shape, shards, -0.22, 0.18) if shards else 1.0
    drawn = jax.random.normal(rng, shape, jnp.float32) * deviation * loudness
    return jnp.minimum(jnp.maximum(drawn, -reach), reach).astype(dtype)


def setup_inputs(seed: int = 0) -> dict:
    seeds = jax.random.split(jax.random.key(seed), 6)
    return {
        "out_grad": centred(seeds[0], (TOKENS, D), 1.0, 6.0, ((0, 16), (1, 32))),
        "inputs": centred(seeds[1], (TOKENS, D), 1.0, 6.0, ((0, 16), (1, 32))),
        "basis_out": centred(seeds[2], (D, KG), D ** -0.5, 0.0625, ((1, 32),)),
        "basis_in": centred(seeds[3], (D, KA), D ** -0.5, 0.0625, ((1, 32),)),
        "correction": jnp.clip(0.5 + 1.5 * jax.random.uniform(seeds[4], (KG, KA), jnp.float32) ** steps_of(seeds[4], (KG, KA), ((0, 32), (1, 16)), -0.2, 0.2), 0.5, 2.0),
    }


def reference(out_grad, inputs, basis_out, basis_in, correction):
    grad_rot = jnp.dot(out_grad, basis_out, preferred_element_type=jnp.float32).astype(jnp.bfloat16)
    input_rot = jnp.dot(inputs, basis_in, preferred_element_type=jnp.float32).astype(jnp.bfloat16)
    half = TOK_DEV // GROUPS
    grad_blocks = grad_rot.reshape(N_CTX, GROUPS, half, KG)
    input_blocks = input_rot.reshape(N_CTX, GROUPS, half, KA)
    total = jnp.zeros((KG, KA), jnp.float32)
    for block in range(GROUPS):
        left = grad_blocks[:, block].reshape(N_CTX * half, KG)
        right = input_blocks[:, block].reshape(N_CTX * half, KA)
        rotated = jnp.dot(left.T, right, preferred_element_type=jnp.float32)
        total = total + rotated * rotated
    return correction + total / TOKENS
```

```python
import functools

import jax
import jax.numpy as jnp
from jax import lax
from jax.experimental import pallas as pl
from jax.experimental.pallas import tpu as pltpu
from jax.sharding import PartitionSpec as P

MESH = pl.DeviceIdType.MESH
GROUPS = 2
CHIPS = 16
CHUNKS = ((0, 80), (80, 64))
N_SEMS = 320
F32 = jnp.float32
BF16 = jnp.bfloat16


def kernel(n_tokens, grad_hbm, in_hbm, bo_hbm, bi_hbm, corr_ref, out_ref, *scratch):
    n_chunks = len(CHUNKS)
    (bo_v, bi_v, sq, sq_in, rot, ssem, rsem, asem, lsem), rest = scratch[:9], scratch[9:]
    x_land, part, part_in, a_ga = rest[:2 * n_chunks], rest[2 * n_chunks:4 * n_chunks], rest[4 * n_chunks:6 * n_chunks], rest[6 * n_chunks:7 * n_chunks]
    a_all, g_all = rest[7 * n_chunks:8 * n_chunks], rest[8 * n_chunks:9 * n_chunks]

    ctx = lax.axis_index("ctx")
    basis = lax.axis_index("basis")
    y, zl = lax.rem(ctx, 8), lax.div(ctx, 8)
    core = lax.rem(basis, 2)
    chip = lax.div(basis, 2)
    x, zh = lax.rem(chip, 4), lax.div(chip, 4)

    def wrap(v, n):
        return lax.rem(v + n, n)

    def chip_of(dz, dx):
        return wrap(zh - dz, 4) * 4 + wrap(x - dx, 4)

    def at_chip(p, k=None):
        return {"ctx": ctx, "basis": p * 2 + (core if k is None else k)}

    def at_ctx(c):
        return {"ctx": c, "basis": basis}

    sibling = at_chip(chip, 1 - core)
    x_up, x_dn = at_chip(chip_of(0, -1)), at_chip(chip_of(0, 1))
    z_up, z_dn = at_chip(chip_of(-1, 0)), at_chip(chip_of(1, 0))
    ctx_at = lambda dy, dz: wrap(zl + dz, 2) * 8 + wrap(y + dy, 8)

    barrier = pltpu.get_barrier_semaphore()
    others = [sibling, x_up, x_dn, z_up, z_dn] + [at_ctx(lax.rem(ctx + r, 16)) for r in range(1, 16)]
    for other in others:
        pl.semaphore_signal(barrier, inc=1, device_id=other, device_id_type=MESH)

    n_sem = [0]
    n_local = [0]
    started = []

    def local(src, dst):
        copy = pltpu.make_async_copy(src, dst, lsem.at[n_local[0]])
        n_local[0] += 1
        copy.start()
        return copy

    def remote(src, dst, device):
        i = n_sem[0]
        n_sem[0] += 1
        copy = pltpu.make_async_remote_copy(
            src_ref=src, dst_ref=dst, send_sem=ssem.at[i], recv_sem=rsem.at[i], device_id=device, device_id_type=MESH
        )
        copy.start()
        started.append(copy)
        return copy

    cols = pl.ds(pl.multiple_of(core * 128, 128), 128)
    b_copies = {}
    for name, hbm, v in (("a", bi_hbm, bi_v), ("g", bo_hbm, bo_v)):
        b_copies[name] = [local(hbm.at[:, core], v.at[:, :, cols])]
    own_copies = []
    for q in range(2 * n_chunks):
        src = (in_hbm, grad_hbm)[q // n_chunks]
        first, n = CHUNKS[q % n_chunks]
        own_copies.append(local(src.at[:, pl.ds(first, n)], x_land[q].at[chip]))

    pl.semaphore_wait(barrier, len(others))

    def gather(own, land, odd, got=lambda dz, dx: None):
        def slot(dz, dx):
            return land.at[chip_of(dz, dx)]

        mine = own if own is not None else slot(0, 0)
        home = slot(0, 0)
        zs = [remote(mine, home, z_up), remote(mine, home, z_dn)]
        yield
        xs = {0: [remote(mine, home, x_up), remote(mine, home, x_dn)]}
        got(0, 0)
        yield
        zs[0].wait_recv()
        zs[1].wait_recv()
        fz = remote(slot(-1, 0), slot(-1, 0), z_dn) if odd else remote(slot(1, 0), slot(1, 0), z_up)
        for dz in (1, -1):
            xs[dz] = [remote(slot(dz, 0), slot(dz, 0), x_up), remote(slot(dz, 0), slot(dz, 0), x_dn)]
        for dz in (1, -1):
            got(dz, 0)
        yield
        fz.wait_recv()
        xs[2] = [remote(slot(2, 0), slot(2, 0), x_up), remote(slot(2, 0), slot(2, 0), x_dn)]
        got(2, 0)
        yield
        fx = {}
        for i, dz in enumerate((0, 1, -1, 2)):
            xs[dz][0].wait_recv()
            xs[dz][1].wait_recv()
            if i % 2:
                fx[dz] = remote(slot(dz, -1), slot(dz, -1), x_dn)
            else:
                fx[dz] = remote(slot(dz, 1), slot(dz, 1), x_up)
            got(dz, 1)
            got(dz, -1)
        yield
        for dz in (0, 1, -1, 2):
            fx[dz].wait_recv()
            got(dz, 2)
        yield

    a_sent = []

    def spread_a(j):
        def got(dz, dx):
            owner = chip_of(dz, dx)
            i = len(a_sent)
            copy = pltpu.make_async_remote_copy(
                src_ref=a_ga[j].at[owner], dst_ref=a_all[j].at[ctx], send_sem=asem.at[i], recv_sem=asem.at[32 * n_chunks + j * 16 + ctx],
                device_id=at_ctx(owner), device_id_type=MESH,
            )
            keep = pltpu.make_async_copy(a_ga[j].at[owner], a_all[j].at[ctx], asem.at[i])
            pl.when(owner != ctx)(copy.start)
            pl.when(owner == ctx)(keep.start)
            a_sent.append((owner, copy, keep))

        return gather(None, a_ga[j], j % 2 == 1, got)

    def spread_g(j):
        up, dn = at_ctx(ctx_at(1, 0)), at_ctx(ctx_at(-1, 0))

        def slot(dy, dz):
            return g_all[j].at[ctx_at(-dy, dz)]

        over = remote(slot(0, 0), slot(0, 0), at_ctx(ctx_at(0, 1)))
        far = (4, 3) if j % 2 else (3, 4)
        ups, dns = {}, {}
        ups[1, 0], dns[1, 0] = remote(slot(0, 0), slot(0, 0), up), remote(slot(0, 0), slot(0, 0), dn)
        over.wait_recv()
        ups[1, 1], dns[1, 1] = remote(slot(0, 1), slot(0, 1), up), remote(slot(0, 1), slot(0, 1), dn)
        yield
        for hop in range(1, 5):
            for dz in (0, 1):
                if hop <= far[0]:
                    ups[hop, dz].wait_recv()
                    if hop < far[0]:
                        ups[hop + 1, dz] = remote(slot(hop, dz), slot(hop, dz), up)
                if hop <= far[1]:
                    dns[hop, dz].wait_recv()
                    if hop < far[1]:
                        dns[hop + 1, dz] = remote(slot(-hop, dz), slot(-hop, dz), dn)
            yield

    swaps = {}

    def rotate(q):
        name = "ag"[q // n_chunks]
        v = (bi_v, bo_v)[q // n_chunks]
        if q % n_chunks == 0:
            b_copies[name][0].wait()
            b_copies[name][1].wait_recv()
        own_copies[q].wait()
        n = CHUNKS[q % n_chunks][1]

        def add(s, total):
            return total + jnp.dot(x_land[q][s].reshape(2 * n, 256), v[s], preferred_element_type=F32)

        total = lax.fori_loop(0, CHIPS, add, jnp.zeros((2 * n, 256), F32))
        part[q][...] = total.reshape(2, n, 256)
        swaps[q] = remote(part[q].at[1 - core], part_in[q], sibling)

    def settle(q):
        j = q % n_chunks
        swaps[q].wait_recv()
        value = (part[q][core] + part_in[q][...]).astype(BF16)
        if q < n_chunks:
            a_ga[j][chip] = value
            return spread_a(j)
        g_all[j][ctx] = value
        return spread_g(j)

    n_q = 2 * n_chunks
    gens = []
    for q in range(n_q):
        src = (in_hbm, grad_hbm)[q // n_chunks]
        first, n = CHUNKS[q % n_chunks]
        gens.append(gather(src.at[:, pl.ds(first, n)], x_land[q], q % 2 == 1))

    def step(g):
        return next(g, "end") != "end"

    step(gens[0])
    step(gens[0])
    for name, hbm, v in (("a", bi_hbm, bi_v), ("g", bo_hbm, bo_v)):
        b_copies[name].append(remote(hbm.at[:, 1 - core], v.at[:, :, cols], sibling))
    side = []

    def advance():
        for g in list(side):
            if not step(g):
                side.remove(g)

    for q in range(n_q):
        step(gens[q])
        if q:
            step(gens[q - 1])
            rotate(q - 1)
        step(gens[q])
        if q + 1 < n_q:
            step(gens[q + 1])
        advance()
        if q:
            side.append(settle(q - 1))
            advance()
        step(gens[q])
        if q + 1 < n_q:
            step(gens[q + 1])
        advance()
        advance()
    step(gens[n_q - 1])
    rotate(n_q - 1)
    side.append(settle(n_q - 1))
    while side:
        advance()

    for owner, copy, keep in a_sent:
        pl.when(owner != ctx)(copy.wait_send)
        pl.when(owner == ctx)(keep.wait)
    rot[...] = jnp.zeros((256, 256), F32)
    for j in range(n_chunks):
        n = CHUNKS[j][1]
        for r in range(1, 16):
            c = lax.rem(ctx + r, 16)
            pltpu.make_async_copy(a_all[j].at[c], a_all[j].at[c], asem.at[32 * n_chunks + j * 16 + c]).wait()

        def multiply(i, _):
            some = pl.ds(i * 4, 4)
            left = g_all[j][some].reshape(4 * n, 256)
            right = a_all[j][some].reshape(4 * n, 256)
            rot[...] += lax.dot_general(left, right, (((0,), (0,)), ((), ())), preferred_element_type=F32)
            return 0

        lax.fori_loop(0, 4, multiply, 0)
    sq[0] = rot[:128] * rot[:128]
    sq[1] = rot[128:] * rot[128:]
    last = remote(sq.at[1 - core], sq_in, sibling)
    last.wait_recv()
    out_ref[...] = corr_ref[...] + (sq[core] + sq_in[...]) / n_tokens
    for copy in started:
        copy.wait_send()


def body(out_grad, inputs, basis_out, basis_in, correction):
    tokens = out_grad.shape[0]
    half = tokens // GROUPS
    any_ = pl.BlockSpec(memory_space=pl.ANY)
    vmem = pl.BlockSpec(memory_space=pltpu.VMEM)
    n_chunks = len(CHUNKS)
    sizes = [n for _, n in CHUNKS]
    scratch = [
        pltpu.VMEM((CHIPS, 256, 256), BF16),
        pltpu.VMEM((CHIPS, 256, 256), BF16),
        pltpu.VMEM((2, 128, 256), F32),
        pltpu.VMEM((128, 256), F32),
        pltpu.VMEM((256, 256), F32),
        pltpu.SemaphoreType.DMA((N_SEMS,)),
        pltpu.SemaphoreType.DMA((N_SEMS,)),
        pltpu.SemaphoreType.DMA((48 * n_chunks,)),
        pltpu.SemaphoreType.DMA((2 + 2 * n_chunks,)),
    ]
    scratch += [pltpu.VMEM((CHIPS, GROUPS, n, 256), BF16) for n in sizes * 2]
    scratch += [pltpu.VMEM((GROUPS, n, 256), F32) for n in sizes * 2]
    scratch += [pltpu.VMEM((n, 256), F32) for n in sizes * 2]
    scratch += [pltpu.VMEM((16, n, 256), BF16) for n in sizes * 3]
    return pl.pallas_call(
        functools.partial(kernel, tokens * lax.axis_size("ctx")),
        name="ekfac",
        out_shape=jax.ShapeDtypeStruct(correction.shape, F32),
        in_specs=[any_] * 4 + [vmem],
        out_specs=vmem,
        scratch_shapes=scratch,
        compiler_params=pltpu.CompilerParams(collective_id=0, has_side_effects=True, vmem_limit_bytes=48 << 20),
        cost_estimate=pl.CostEstimate(flops=3 * 10**9, bytes_accessed=5 * 10**6, transcendentals=0),
    )(
        out_grad.reshape(GROUPS, half, 256),
        inputs.reshape(GROUPS, half, 256),
        basis_out.reshape(CHIPS, 2, 256, 128),
        basis_in.reshape(CHIPS, 2, 256, 128),
        correction,
    )


def solution(mesh):
    return jax.shard_map(
        body,
        mesh=mesh,
        in_specs=(P("ctx", "basis"), P("ctx", "basis"), P(None, "basis"), P(None, "basis"), P("basis", "ctx")),
        out_specs=P("basis", "ctx"),
        check_vma=False,
    )
```

```python
import jax
import jax.numpy as jnp
from jax import lax
from jax.experimental import pallas as pl
from jax.experimental.pallas import tpu as pltpu
from jax.sharding import PartitionSpec as P

MESH = pl.DeviceIdType.MESH
GROUPS = 2
CHIPS = 16
CHUNKS = ((0, 80), (80, 64))
N_SEMS = 90
F32 = jnp.float32
BF16 = jnp.bfloat16


def schedule(n):
    h = n // 2
    done = {}
    steps = []

    def add(op, q, upto=None):
        if 0 <= q < (h if op in "mg" else n):
            while upto is None or done.get((op, q), 0) < upto:
                steps.append((op, q))
                done[op, q] = done.get((op, q), 0) + 1
                if upto is None:
                    break

    add("x", 0, 2)
    add("x", 1, 1)
    steps.append(("b", 0))
    for q in range(n + 1):
        add("x", q, 3)
        add("x", q - 1, 6)
        add("r", q - 1)
        add("x", q, 4)
        add("x", q + 1, 1)
        add("m", q - 2, 3)
        add("s", q - 1)
        add("m", q - 1, 2)
        add("g", q - 1 - h, 1)
        add("m", q - 2, 4)
        add("x", q, 5)
        add("x", q + 1, 2)
        add("m", q - 2, 6)
        add("m", q - 1, 3)
        add("g", q - 2 - h, 9)
    return steps + [("m", j) for j in range(h) for _ in range(7 - done["m", j])] + [("g", j) for j in range(h) for _ in range(6)]


def kernel(grad_hbm, in_hbm, bo_hbm, bi_hbm, out_ref, *scratch):
    n_chunks = len(CHUNKS)
    n_q = 2 * n_chunks
    (bo_v, bi_v, sq, sq_in, rot, rot_in, sems), rest = scratch[:7], scratch[7:]
    x_land, part, part_in = rest[:n_q], rest[n_q:2 * n_q], rest[2 * n_q:3 * n_q]
    a_ga, a_all, g_all = (rest[3 * n_q + i * n_chunks:3 * n_q + (i + 1) * n_chunks] for i in range(3))

    ctx = lax.axis_index("ctx")
    basis = lax.axis_index("basis")
    y, zl = lax.rem(ctx, 8), lax.div(ctx, 8)
    core = lax.rem(basis, 2)
    chip = lax.div(basis, 2)
    x, zh = lax.rem(chip, 4), lax.div(chip, 4)

    def wrap(v, n):
        return lax.rem(v + n, n)

    def chip_of(dz, dx):
        return wrap(zh - dz, 4) * 4 + wrap(x - dx, 4)

    def at_chip(p, k):
        return {"ctx": ctx, "basis": p * 2 + k}

    def at_ctx(c):
        return {"ctx": c, "basis": basis}

    def ctx_of(dy, dz):
        return wrap(zl - dz, 2) * 8 + wrap(y - dy, 8)

    sibling = at_chip(chip, 1 - core)
    x_up, x_dn = at_chip(chip_of(0, -1), core), at_chip(chip_of(0, 1), core)
    z_up, z_dn = at_chip(chip_of(-1, 0), core), at_chip(chip_of(1, 0), core)
    peers = [at_ctx(ctx_of(-r, 0)) for r in range(1, 8)]
    over = at_ctx(ctx_of(0, 1))

    barrier = pltpu.get_barrier_semaphore()
    others = [sibling, over, x_up, x_dn, z_up, z_dn] + peers
    for other in others:
        pl.semaphore_signal(barrier, inc=1, device_id=other, device_id_type=MESH)

    used = [0]
    at_end = []

    def new():
        used[0] += 1
        return sems.at[used[0] - 1]

    def take(sem, ref):
        pltpu.make_async_copy(ref, ref, sem).wait()

    def local(src, dst):
        copy = pltpu.make_async_copy(src, dst, new())
        copy.start()
        return copy

    def remote(src, dst, device, send, recv):
        copy = pltpu.make_async_remote_copy(
            src_ref=src, dst_ref=dst, send_sem=send, recv_sem=recv, device_id=device, device_id_type=MESH
        )
        copy.start()
        return copy

    def swap(src, dst):
        copy = remote(src, dst, sibling, new(), new())
        at_end.append(copy.wait_send)
        return copy

    cols = pl.ds(pl.multiple_of(core * 128, 128), 128)
    b_copies = [[local(hbm.at[:, core], v.at[:, :, cols])] for hbm, v in ((bi_hbm, bi_v), (bo_hbm, bo_v))]
    shards, own_copies = [], []
    for q in range(n_q):
        first, n = CHUNKS[q % n_chunks]
        shards.append((in_hbm, grad_hbm)[q // n_chunks].at[:, pl.ds(first, n)])
        own_copies.append(local(shards[q], x_land[q].at[chip]))

    pl.semaphore_wait(barrier, len(others))

    def gather(own, land, odd, got=lambda dz, dx: None):
        send, z1, z2, x2 = (new() for _ in range(4))
        x1 = {dz: new() for dz in (0, 1, -1, 2)}

        def slot(dz, dx):
            return land.at[chip_of(dz, dx)]

        def hop(dz, dx, device, recv, src=None, part=None):
            dst = slot(dz, dx)
            if part is not None:
                dst = dst.at[part]
            remote(dst if src is None else src, dst, device, send, recv)

        hop(0, 0, z_up, z1, own)
        hop(0, 0, z_dn, z1, own)
        yield
        hop(0, 0, x_up, x1[0], own)
        hop(0, 0, x_dn, x1[0], own)
        got(0, 0)
        yield
        take(z1, land.at[pl.ds(0, 2)])
        if land.ndim == 4:
            hop(1, 0, z_up, z2, part=0)
            hop(-1, 0, z_dn, z2, part=1)
        elif odd:
            hop(-1, 0, z_dn, z2)
        else:
            hop(1, 0, z_up, z2)
        for dz in (1, -1):
            hop(dz, 0, x_up, x1[dz])
            hop(dz, 0, x_dn, x1[dz])
        got(1, 0)
        got(-1, 0)
        yield
        take(z2, land.at[0])
        hop(2, 0, x_up, x1[2])
        hop(2, 0, x_dn, x1[2])
        got(2, 0)
        yield
        for i, dz in enumerate((0, 1, -1, 2)):
            take(x1[dz], land.at[pl.ds(0, 2)])
            if i % 2:
                hop(dz, -1, x_dn, x2)
            else:
                hop(dz, 1, x_up, x2)
            got(dz, 1)
            got(dz, -1)
        yield
        take(x2, land.at[pl.ds(0, 4)])
        for dz in (0, 1, -1, 2):
            got(dz, 2)
        at_end.append(lambda: take(send, land.at[pl.ds(0, 15)]))
        yield

    def spread_a(j):
        send, recv, kept = new(), new(), new()

        def got(dz, dx):
            owner = chip_of(dz, dx)
            target = lax.rem(owner, 8)
            src, dst = a_ga[j].at[owner], a_all[j].at[lax.div(owner, 8), y]

            @pl.when(target != y)
            def _():
                remote(src, dst, at_ctx(zl * 8 + target), send, recv)

            @pl.when(target == y)
            def _():
                pltpu.make_async_copy(src, dst, kept).start()

        yield from gather(a_ga[j].at[chip], a_ga[j], j % 2 == 1, got)
        take(recv, a_ga[j].at[pl.ds(0, 14)])
        take(kept, a_ga[j].at[pl.ds(0, 2)])
        at_end.append(lambda: take(send, a_ga[j].at[pl.ds(0, 14)]))
        yield

    def spread_g(j):
        here = g_all[j].at[y]
        send, recv = new(), new()
        for peer in peers:
            remote(here, here, peer, send, recv)
        yield
        take(recv, g_all[j].at[pl.ds(0, 7)])
        at_end.append(lambda: take(send, g_all[j].at[pl.ds(0, 7)]))
        yield

    swaps = {}

    def rotate(q):
        v = (bi_v, bo_v)[q // n_chunks]
        if q % n_chunks == 0:
            own, other = b_copies[q // n_chunks]
            own.wait()
            other.wait_recv()
        own_copies[q].wait()
        n = CHUNKS[q % n_chunks][1]

        def add(s, total):
            return total + jnp.dot(x_land[q][s].reshape(2 * n, 256), v[s], preferred_element_type=F32)

        total = lax.fori_loop(0, CHIPS, add, jnp.zeros((2 * n, 256), F32))
        part[q][...] = total.reshape(2, n, 256)
        swaps[q] = swap(part[q].at[1 - core], part_in[q])

    def settle(q):
        j = q % n_chunks
        swaps[q].wait_recv()
        value = (part[q][core] + part_in[q][...]).astype(BF16)
        if q < n_chunks:
            a_ga[j][chip] = value
            gens["m", j] = spread_a(j)
        else:
            g_all[j][y] = value
            gens["g", j] = spread_g(j)

    gens = {("x", q): gather(shards[q], x_land[q], q % 2 == 1) for q in range(n_q)}
    for op, q in schedule(n_q):
        if op in "xmg":
            next(gens[op, q], None)
        elif op == "r":
            rotate(q)
        elif op == "s":
            settle(q)
        else:
            for copies, hbm, v in ((b_copies[0], bi_hbm, bi_v), (b_copies[1], bo_hbm, bo_v)):
                copies.append(swap(hbm.at[:, 1 - core], v.at[:, :, cols]))

    def multiply(j):
        n = CHUNKS[j][1]

        def add(i, _):
            some = pl.ds(i * 4, 4)
            left = g_all[j][some].reshape(4 * n, 256)
            for h in range(2):
                right = a_all[j][h, some].reshape(4 * n, 256)
                rot[h] += lax.dot_general(left, right, (((0,), (0,)), ((), ())), preferred_element_type=F32)
            return 0

        lax.fori_loop(0, 2, add, 0)

    rot[...] = jnp.zeros((2, 256, 256), F32)
    for j in range(n_chunks):
        multiply(j)
    halves = [pl.ds(pl.multiple_of((1 - core) * 128, 128), 128), pl.ds(pl.multiple_of(core * 128, 128), 128)]
    parts = [remote(rot.at[1 - zl, half], rot_in.at[half], over, new(), new()) for half in halves]
    at_end.extend(p.wait_send for p in parts)

    def square(i):
        parts[i].wait_recv()
        value = rot[zl, halves[i], :] + rot_in[halves[i], :]
        return value * value

    sq[...] = square(0)
    last = swap(sq, sq_in)
    mine = square(1)
    last.wait_recv()
    out_ref[...] = mine + sq_in[...]
    for finish in at_end:
        finish()


def body(out_grad, inputs, basis_out, basis_in, correction):
    tokens = out_grad.shape[0]
    half = tokens // GROUPS
    n_chunks = len(CHUNKS)
    sizes = [n for _, n in CHUNKS]
    scratch = [
        pltpu.VMEM((CHIPS, 256, 256), BF16),
        pltpu.VMEM((CHIPS, 256, 256), BF16),
        pltpu.VMEM((128, 256), F32),
        pltpu.VMEM((128, 256), F32),
        pltpu.VMEM((2, 256, 256), F32),
        pltpu.VMEM((256, 256), F32),
        pltpu.SemaphoreType.DMA((N_SEMS,)),
    ]
    scratch += [pltpu.VMEM((CHIPS, GROUPS, n, 256), BF16) for n in sizes * 2]
    scratch += [pltpu.VMEM((GROUPS, n, 256), F32) for n in sizes * 2]
    scratch += [pltpu.VMEM((n, 256), F32) for n in sizes * 2]
    scratch += [pltpu.VMEM((CHIPS, n, 256), BF16) for n in sizes]
    scratch += [pltpu.VMEM((2, 8, n, 256), BF16) for n in sizes]
    scratch += [pltpu.VMEM((8, n, 256), BF16) for n in sizes]
    squares = pl.pallas_call(
        kernel,
        name="ekfac",
        out_shape=jax.ShapeDtypeStruct(correction.shape, F32),
        in_specs=[pl.BlockSpec(memory_space=pl.ANY)] * 4,
        out_specs=pl.BlockSpec(memory_space=pltpu.VMEM),
        scratch_shapes=scratch,
        compiler_params=pltpu.CompilerParams(collective_id=0, has_side_effects=True, vmem_limit_bytes=62 << 20),
        cost_estimate=pl.CostEstimate(flops=3 * 10**9, bytes_accessed=5 * 10**6, transcendentals=0),
    )(
        out_grad.reshape(GROUPS, half, 256),
        inputs.reshape(GROUPS, half, 256),
        basis_out.reshape(CHIPS, 2, 256, 128),
        basis_in.reshape(CHIPS, 2, 256, 128),
    )
    return correction + squares / (tokens * lax.axis_size("ctx"))


def solution(mesh):
    return jax.shard_map(
        body,
        mesh=mesh,
        in_specs=(P("ctx", "basis"), P("ctx", "basis"), P(None, "basis"), P(None, "basis"), P("basis", "ctx")),
        out_specs=P("basis", "ctx"),
        check_vma=False,
    )
```

```python
import jax
import jax.numpy as jnp
from jax import lax
from jax.experimental import pallas as pl
from jax.experimental.pallas import tpu as pltpu
from jax.sharding import PartitionSpec as P

MESH = pl.DeviceIdType.MESH
GROUPS = 2
CHIPS = 16
CHUNKS = (((0, 80), (80, 64)), ((0, 80), (80, 64)))
ORDER = (
    "x0", "x1", "x0", "x1", "b0", "x0", "x1", "x0", "x1", "x2", "x3", "x0", "x1", "x2", "x3", "x0",
    "r0", "s0", "m0", "m0", "x1", "r1", "s1", "m1", "m1", "x2", "m0", "m1", "x2", "m0", "m1", "m0",
    "m1", "x3", "x3", "x2", "m0", "m1", "x3", "x2", "r2", "s2", "g0", "g0", "x3", "r3", "s3", "g1",
    "g0", "g0", "m0", "m1", "g0", "f0", "g1", "f1",
)
N_SEMS = 110
F32 = jnp.float32
BF16 = jnp.bfloat16


def kernel(grad_hbm, in_hbm, bo_hbm, bi_hbm, out_ref, *scratch):
    n_a, n_g = (len(c) for c in CHUNKS)
    n_q = n_a + n_g
    pieces = CHUNKS[0] + CHUNKS[1]
    (bo_v, bi_v, sq, sq_in, rot, rot_in, sems), rest = scratch[:7], scratch[7:]
    x_land, part, part_in = rest[:n_q], rest[n_q:2 * n_q], rest[2 * n_q:3 * n_q]
    a_ga, g_mine, a_all, g_all = rest[3 * n_q:3 * n_q + n_a], rest[3 * n_q + n_a:4 * n_q], rest[4 * n_q], rest[4 * n_q + 1]

    ctx = lax.axis_index("ctx")
    basis = lax.axis_index("basis")
    y, zl = lax.rem(ctx, 8), lax.div(ctx, 8)
    core = lax.rem(basis, 2)
    chip = lax.div(basis, 2)
    x, zh = lax.rem(chip, 4), lax.div(chip, 4)

    def wrap(v, n):
        return lax.rem(v + n, n)

    def chip_of(dz, dx):
        return wrap(zh - dz, 4) * 4 + wrap(x - dx, 4)

    def at_chip(p, k):
        return {"ctx": ctx, "basis": p * 2 + k}

    def at_ctx(c):
        return {"ctx": c, "basis": basis}

    def ctx_of(dy, dz):
        return wrap(zl - dz, 2) * 8 + wrap(y - dy, 8)

    sibling = at_chip(chip, 1 - core)
    x_up, x_dn = at_chip(chip_of(0, -1), core), at_chip(chip_of(0, 1), core)
    z_up, z_dn = at_chip(chip_of(-1, 0), core), at_chip(chip_of(1, 0), core)
    peers = [at_ctx(ctx_of(-r, 0)) for r in range(1, 8)]
    over = at_ctx(ctx_of(0, 1))

    barrier = pltpu.get_barrier_semaphore()
    others = [sibling, over, x_up, x_dn, z_up, z_dn] + peers
    for other in others:
        pl.semaphore_signal(barrier, inc=1, device_id=other, device_id_type=MESH)

    used = [0]
    at_end = []

    def new():
        used[0] += 1
        return sems.at[used[0] - 1]

    def take(sem, ref):
        pltpu.make_async_copy(ref, ref, sem).wait()

    def local(src, dst):
        copy = pltpu.make_async_copy(src, dst, new())
        copy.start()
        return copy

    def remote(src, dst, device, send, recv):
        copy = pltpu.make_async_remote_copy(
            src_ref=src, dst_ref=dst, send_sem=send, recv_sem=recv, device_id=device, device_id_type=MESH
        )
        copy.start()
        return copy

    def swap(src, dst):
        copy = remote(src, dst, sibling, new(), new())
        at_end.append(copy.wait_send)
        return copy

    cols = pl.ds(pl.multiple_of(core * 128, 128), 128)
    b_copies = [[local(hbm.at[:, core], v.at[:, :, cols])] for hbm, v in ((bi_hbm, bi_v), (bo_hbm, bo_v))]
    shards, own_copies = [], []
    for q in range(n_q):
        shards.append((in_hbm if q < n_a else grad_hbm).at[:, pl.ds(*pieces[q])])
        own_copies.append(local(shards[q], x_land[q].at[chip]))

    pl.semaphore_wait(barrier, len(others))

    def gather(own, land, odd, got=lambda dz, dx: None):
        send, z1, z2, x2 = (new() for _ in range(4))
        x1 = {dz: new() for dz in (0, 1, -1, 2)}

        def slot(dz, dx):
            return land.at[chip_of(dz, dx)]

        def hop(dz, dx, device, recv, src=None, part=None):
            dst = slot(dz, dx)
            if part is not None:
                dst = dst.at[part]
            remote(dst if src is None else src, dst, device, send, recv)

        hop(0, 0, z_up, z1, own)
        hop(0, 0, z_dn, z1, own)
        yield
        hop(0, 0, x_up, x1[0], own)
        hop(0, 0, x_dn, x1[0], own)
        got(0, 0)
        yield
        take(z1, land.at[pl.ds(0, 2)])
        if land.ndim == 4:
            hop(1, 0, z_up, z2, part=0)
            hop(-1, 0, z_dn, z2, part=1)
        elif odd:
            hop(-1, 0, z_dn, z2)
        else:
            hop(1, 0, z_up, z2)
        for dz in (1, -1):
            hop(dz, 0, x_up, x1[dz])
            hop(dz, 0, x_dn, x1[dz])
        got(1, 0)
        got(-1, 0)
        yield
        take(z2, land.at[0])
        hop(2, 0, x_up, x1[2])
        hop(2, 0, x_dn, x1[2])
        got(2, 0)
        yield
        for i, dz in enumerate((0, 1, -1, 2)):
            take(x1[dz], land.at[pl.ds(0, 2)])
            if i % 2:
                hop(dz, -1, x_dn, x2)
            else:
                hop(dz, 1, x_up, x2)
            got(dz, 1)
            got(dz, -1)
        yield
        take(x2, land.at[pl.ds(0, 4)])
        for dz in (0, 1, -1, 2):
            got(dz, 2)
        at_end.append(lambda: take(send, land.at[pl.ds(0, 15)]))
        yield

    def spread_a(j):
        send, recv, kept = new(), new(), new()

        def got(dz, dx):
            owner = chip_of(dz, dx)
            target = lax.rem(owner, 8)
            src, dst = a_ga[j].at[owner], a_all.at[lax.div(owner, 8), y, pl.ds(*CHUNKS[0][j])]

            @pl.when(target != y)
            def _():
                remote(src, dst, at_ctx(zl * 8 + target), send, recv)

            @pl.when(target == y)
            def _():
                pltpu.make_async_copy(src, dst, kept).start()

        yield from gather(a_ga[j].at[chip], a_ga[j], j % 2 == 1, got)
        take(recv, a_ga[j].at[pl.ds(0, 14)])
        take(kept, a_ga[j].at[pl.ds(0, 2)])
        at_end.append(lambda: take(send, a_ga[j].at[pl.ds(0, 14)]))
        yield

    def spread_g(j):
        rows = pl.ds(*CHUNKS[1][j])
        here = g_all.at[y, rows]
        send = new()
        if j + 1 < n_g:
            hops = [new() for _ in range(4)]
            up, dn = peers[0], peers[6]

            def hop(i):
                above, below = (g_all.at[lax.rem(y + 8 + d, 8), rows] for d in (-i, i))
                if i < 4:
                    remote(above if i else g_mine[j], above, up, send, hops[i])
                if i < 3:
                    remote(below if i else g_mine[j], below, dn, send, hops[i])

            hop(0)
            yield
            for i in range(1, 4):
                take(hops[i - 1], g_all.at[pl.ds(0, 2), rows])
                hop(i)
                yield
            take(hops[3], g_all.at[0, rows])
        else:
            recv = new()
            for peer in peers:
                remote(g_mine[j], here, peer, send, recv)
            yield
            take(recv, g_all.at[pl.ds(0, 7), rows])
        at_end.append(lambda: take(send, g_all.at[pl.ds(0, 7), rows]))
        yield

    swaps = {}

    def rotate(q):
        i = 0 if q < n_a else 1
        v = (bi_v, bo_v)[i]
        if q in (0, n_a):
            own, other = b_copies[i]
            own.wait()
            other.wait_recv()
        own_copies[q].wait()
        n = pieces[q][1]

        def add(i, total):
            for s in range(4):
                s += 4 * i
                total += jnp.dot(x_land[q][s].reshape(2 * n, 256), v[s], preferred_element_type=F32)
            return total

        total = lax.fori_loop(0, CHIPS // 4, add, jnp.zeros((2 * n, 256), F32))
        part[q][...] = total.reshape(2, n, 256)
        swaps[q] = swap(part[q].at[1 - core], part_in[q])

    def settle(q):
        swaps[q].wait_recv()
        value = (part[q][core] + part_in[q][...]).astype(BF16)
        if q < n_a:
            a_ga[q][chip] = value
            gens["m", q] = spread_a(q)
        else:
            j = q - n_a
            g_mine[j][...] = value
            g_all[y, pl.ds(*pieces[q]), :] = value
            gens["g", j] = spread_g(j)

    def multiply(j):
        first, n = CHUNKS[1][j]
        rows = pl.ds(first, n)

        def add(i, _):
            some = pl.ds(i * 4, 4)
            left = g_all[some, rows, :].reshape(4 * n, 256)
            for h in range(2):
                right = a_all[h, some, rows, :].reshape(4 * n, 256)
                rot[h] += lax.dot_general(left, right, (((0,), (0,)), ((), ())), preferred_element_type=F32)
            return 0

        lax.fori_loop(0, 2, add, 0)

    gens = {("x", q): gather(shards[q], x_land[q], q % 2 == 1) for q in range(n_q)}
    rot[...] = jnp.zeros((2, 256, 256), F32)
    for step in ORDER:
        op, q = step[0], int(step[1])
        if op in "xmg":
            next(gens[op, q])
        elif op == "r":
            rotate(q)
        elif op == "s":
            settle(q)
        elif op == "f":
            multiply(q)
        else:
            for copies, hbm, v in ((b_copies[0], bi_hbm, bi_v), (b_copies[1], bo_hbm, bo_v)):
                copies.append(swap(hbm.at[:, 1 - core], v.at[:, :, cols]))
    halves = [pl.ds(pl.multiple_of((1 - core) * 128, 128), 128), pl.ds(pl.multiple_of(core * 128, 128), 128)]
    parts = [remote(rot.at[1 - zl, half], rot_in.at[half], over, new(), new()) for half in halves]
    at_end.extend(p.wait_send for p in parts)

    def square(i):
        parts[i].wait_recv()
        value = rot[zl, halves[i], :] + rot_in[halves[i], :]
        return value * value

    sq[...] = square(0)
    last = swap(sq, sq_in)
    mine = square(1)
    last.wait_recv()
    out_ref[...] = mine + sq_in[...]
    for finish in at_end:
        finish()


def body(out_grad, inputs, basis_out, basis_in, correction):
    tokens = out_grad.shape[0]
    half = tokens // GROUPS
    sizes = [[n for _, n in c] for c in CHUNKS]
    both = sizes[0] + sizes[1]
    scratch = [
        pltpu.VMEM((CHIPS, 256, 256), BF16),
        pltpu.VMEM((CHIPS, 256, 256), BF16),
        pltpu.VMEM((128, 256), F32),
        pltpu.VMEM((128, 256), F32),
        pltpu.VMEM((2, 256, 256), F32),
        pltpu.VMEM((256, 256), F32),
        pltpu.SemaphoreType.DMA((N_SEMS,)),
    ]
    scratch += [pltpu.VMEM((CHIPS, GROUPS, n, 256), BF16) for n in both]
    scratch += [pltpu.VMEM((GROUPS, n, 256), F32) for n in both]
    scratch += [pltpu.VMEM((n, 256), F32) for n in both]
    scratch += [pltpu.VMEM((CHIPS, n, 256), BF16) for n in sizes[0]]
    scratch += [pltpu.VMEM((n, 256), BF16) for n in sizes[1]]
    scratch += [pltpu.VMEM((2, 8, half, 256), BF16), pltpu.VMEM((8, half, 256), BF16)]
    squares = pl.pallas_call(
        kernel,
        name="ekfac",
        out_shape=jax.ShapeDtypeStruct(correction.shape, F32),
        in_specs=[pl.BlockSpec(memory_space=pl.ANY)] * 4,
        out_specs=pl.BlockSpec(memory_space=pltpu.VMEM),
        scratch_shapes=scratch,
        compiler_params=pltpu.CompilerParams(collective_id=0, has_side_effects=True, vmem_limit_bytes=62 << 20),
        cost_estimate=pl.CostEstimate(flops=3 * 10**9, bytes_accessed=5 * 10**6, transcendentals=0),
    )(
        out_grad.reshape(GROUPS, half, 256),
        inputs.reshape(GROUPS, half, 256),
        basis_out.reshape(CHIPS, 2, 256, 128),
        basis_in.reshape(CHIPS, 2, 256, 128),
    )
    return correction + squares / (tokens * lax.axis_size("ctx"))


def solution(mesh):
    return jax.shard_map(
        body,
        mesh=mesh,
        in_specs=(P("ctx", "basis"), P("ctx", "basis"), P(None, "basis"), P(None, "basis"), P("basis", "ctx")),
        out_specs=P("basis", "ctx"),
        check_vma=False,
    )
```

```python
import jax
import jax.numpy as jnp
from jax import lax
from jax.experimental import pallas as pl
from jax.experimental.pallas import tpu as pltpu
from jax.sharding import PartitionSpec as P

MESH = pl.DeviceIdType.MESH
GROUPS = 2
CHIPS = 16
CHUNKS = (((0, 80), (80, 64)), ((0, 80), (80, 64)))
ORDER = (
    "x0", "x1", "x0", "x1", "b0", "x0", "x1", "x0", "x1", "x0", "x1", "x2", "x3", "x0", "r0", "x1",
    "r1", "s0", "m0", "m0", "s1", "m1", "m1", "x2", "x3", "m0", "m1", "m0", "m1", "m0", "m1", "x2",
    "x3", "x2", "x3", "m0", "m1", "x2", "x3", "x2", "r2", "s2", "g0", "x3", "r3", "g0", "s3", "g1",
    "g0", "g0", "m0", "m1", "g0", "f0", "g1",
)
N_SEMS = 85
F32 = jnp.float32
BF16 = jnp.bfloat16


def kernel(grad_hbm, in_hbm, bo_hbm, bi_hbm, out_ref, *scratch):
    n_a, n_g = (len(c) for c in CHUNKS)
    n_q = n_a + n_g
    pieces = CHUNKS[0] + CHUNKS[1]
    (bo_v, bi_v, sq, sq_in, rot, rot_in, sems), rest = scratch[:7], scratch[7:]
    x_land, part, part_in = rest[:n_q], rest[n_q:2 * n_q], rest[2 * n_q:3 * n_q]
    a_ga, g_mine, a_all, g_all = rest[3 * n_q:3 * n_q + n_a], rest[3 * n_q + n_a:4 * n_q], rest[4 * n_q], rest[4 * n_q + 1]

    ctx = lax.axis_index("ctx")
    basis = lax.axis_index("basis")
    y, zl = lax.rem(ctx, 8), lax.div(ctx, 8)
    core = lax.rem(basis, 2)
    chip = lax.div(basis, 2)
    x, zh = lax.rem(chip, 4), lax.div(chip, 4)

    def wrap(v, n):
        return lax.rem(v + n, n)

    def chip_of(dz, dx):
        return wrap(zh - dz, 4) * 4 + wrap(x - dx, 4)

    def at_chip(p, k):
        return {"ctx": ctx, "basis": p * 2 + k}

    def at_ctx(c):
        return {"ctx": c, "basis": basis}

    def ctx_of(dy, dz):
        return wrap(zl - dz, 2) * 8 + wrap(y - dy, 8)

    sibling = at_chip(chip, 1 - core)
    x_up, x_dn = at_chip(chip_of(0, -1), core), at_chip(chip_of(0, 1), core)
    z_up, z_dn = at_chip(chip_of(-1, 0), core), at_chip(chip_of(1, 0), core)
    peers = [at_ctx(ctx_of(-r, 0)) for r in range(1, 8)]
    over = at_ctx(ctx_of(0, 1))

    barrier = pltpu.get_barrier_semaphore()
    others = [sibling, over, x_up, x_dn, z_up, z_dn] + peers
    for other in others:
        pl.semaphore_signal(barrier, inc=1, device_id=other, device_id_type=MESH)

    used = [0]
    at_end = []

    def new():
        used[0] += 1
        return sems.at[used[0] - 1]

    def take(sem, ref):
        pltpu.make_async_copy(ref, ref, sem).wait()

    def local(src, dst):
        copy = pltpu.make_async_copy(src, dst, new())
        copy.start()
        return copy

    def remote(src, dst, device, send, recv):
        copy = pltpu.make_async_remote_copy(
            src_ref=src, dst_ref=dst, send_sem=send, recv_sem=recv, device_id=device, device_id_type=MESH
        )
        copy.start()
        return copy

    def swap(src, dst):
        copy = remote(src, dst, sibling, new(), new())
        at_end.append(copy.wait_send)
        return copy

    cols = pl.ds(pl.multiple_of(core * 128, 128), 128)
    b_copies = [[local(hbm.at[:, core], v.at[:, :, cols])] for hbm, v in ((bi_hbm, bi_v), (bo_hbm, bo_v))]
    shards, own_copies = [], []
    for q in range(n_q):
        shards.append((in_hbm if q < n_a else grad_hbm).at[:, pl.ds(*pieces[q])])
        own_copies.append(local(shards[q], x_land[q].at[chip]))

    pl.semaphore_wait(barrier, len(others))

    def gather(own, land, odd, got=lambda dz, dx: None):
        send, z1, z2, x2 = (new() for _ in range(4))
        x1 = {dz: new() for dz in (0, 1, -1, 2)}

        def slot(dz, dx):
            return land.at[chip_of(dz, dx)]

        def hop(dz, dx, device, recv, src=None, part=None):
            dst = slot(dz, dx)
            if part is not None:
                dst = dst.at[part]
            remote(dst if src is None else src, dst, device, send, recv)

        hop(0, 0, z_up, z1, own)
        hop(0, 0, z_dn, z1, own)
        yield
        hop(0, 0, x_up, x1[0], own)
        hop(0, 0, x_dn, x1[0], own)
        got(0, 0)
        yield
        take(z1, land.at[pl.ds(0, 2)])
        if land.ndim == 4:
            hop(1, 0, z_up, z2, part=0)
            hop(-1, 0, z_dn, z2, part=1)
        elif odd:
            hop(-1, 0, z_dn, z2)
        else:
            hop(1, 0, z_up, z2)
        for dz in (1, -1):
            hop(dz, 0, x_up, x1[dz])
            hop(dz, 0, x_dn, x1[dz])
        got(1, 0)
        got(-1, 0)
        yield
        take(z2, land.at[0])
        hop(2, 0, x_up, x1[2])
        hop(2, 0, x_dn, x1[2])
        got(2, 0)
        yield
        for i, dz in enumerate((0, 1, -1, 2)):
            take(x1[dz], land.at[pl.ds(0, 2)])
            if i % 2:
                hop(dz, -1, x_dn, x2)
            else:
                hop(dz, 1, x_up, x2)
            got(dz, 1)
            got(dz, -1)
        yield
        take(x2, land.at[pl.ds(0, 4)])
        for dz in (0, 1, -1, 2):
            got(dz, 2)
        at_end.append(lambda: take(send, land.at[pl.ds(0, 15)]))
        yield

    def spread_a(j):
        send, recv, kept = new(), new(), new()

        def got(dz, dx):
            owner = chip_of(dz, dx)
            target = lax.rem(owner, 8)
            src, dst = a_ga[j].at[owner], a_all.at[lax.div(owner, 8), y, pl.ds(*CHUNKS[0][j])]

            @pl.when(target != y)
            def _():
                remote(src, dst, at_ctx(zl * 8 + target), send, recv)

            @pl.when(target == y)
            def _():
                pltpu.make_async_copy(src, dst, kept).start()

        yield from gather(a_ga[j].at[chip], a_ga[j], j % 2 == 1, got)
        take(recv, a_ga[j].at[pl.ds(0, 14)])
        take(kept, a_ga[j].at[pl.ds(0, 2)])
        at_end.append(lambda: take(send, a_ga[j].at[pl.ds(0, 14)]))
        yield

    def spread_g(j):
        rows = pl.ds(*CHUNKS[1][j])
        here = g_all.at[y, rows]
        send = new()
        if j + 1 < n_g:
            hops = [new() for _ in range(4)]
            up, dn = peers[0], peers[6]

            def hop(i):
                above, below = (g_all.at[lax.rem(y + 8 + d, 8), rows] for d in (-i, i))
                if i < 4:
                    remote(above if i else g_mine[j], above, up, send, hops[i])
                if i < 3:
                    remote(below if i else g_mine[j], below, dn, send, hops[i])

            hop(0)
            yield
            for i in range(1, 4):
                take(hops[i - 1], g_all.at[pl.ds(0, 2), rows])
                hop(i)
                yield
            take(hops[3], g_all.at[0, rows])
        else:
            recv = new()
            for peer in peers:
                remote(g_mine[j], here, peer, send, recv)
            yield
            take(recv, g_all.at[pl.ds(0, 7), rows])
        at_end.append(lambda: take(send, g_all.at[pl.ds(0, 7), rows]))
        yield

    swaps = {}

    def rotate(q):
        i = 0 if q < n_a else 1
        v = (bi_v, bo_v)[i]
        if q in (0, n_a):
            own, other = b_copies[i]
            own.wait()
            other.wait_recv()
        own_copies[q].wait()
        n = pieces[q][1]

        def add(i, total):
            for s in range(4):
                s += 4 * i
                total += jnp.dot(x_land[q][s].reshape(2 * n, 256), v[s], preferred_element_type=F32)
            return total

        total = lax.fori_loop(0, CHIPS // 4, add, jnp.zeros((2 * n, 256), F32))
        part[q][...] = total.reshape(2, n, 256)
        swaps[q] = swap(part[q].at[1 - core], part_in[q])

    def settle(q):
        swaps[q].wait_recv()
        value = (part[q][core] + part_in[q][...]).astype(BF16)
        if q < n_a:
            a_ga[q][chip] = value
            gens["m", q] = spread_a(q)
        else:
            j = q - n_a
            g_mine[j][...] = value
            g_all[y, pl.ds(*pieces[q]), :] = value
            gens["g", j] = spread_g(j)

    def multiply(j, tiles):
        first, n = CHUNKS[1][j]
        rows = pl.ds(first, n)

        def add(i, _):
            some = pl.ds(i * 4, 4)
            left = g_all[some, rows, :].reshape(4 * n, 256)
            for h in tiles:
                right = a_all[h, some, rows, :].reshape(4 * n, 256)
                rot[h] += lax.dot_general(left, right, (((0,), (0,)), ((), ())), preferred_element_type=F32)
            return 0

        lax.fori_loop(0, 2, add, 0)

    gens = {("x", q): gather(shards[q], x_land[q], q % 2 == 1) for q in range(n_q)}
    rot[...] = jnp.zeros((2, 256, 256), F32)
    for step in ORDER:
        op, q = step[0], int(step[1])
        if op in "xmg":
            next(gens[op, q])
        elif op == "r":
            rotate(q)
        elif op == "s":
            settle(q)
        elif op == "f":
            multiply(q, (0, 1))
        else:
            for copies, hbm, v in ((b_copies[0], bi_hbm, bi_v), (b_copies[1], bo_hbm, bo_v)):
                copies.append(swap(hbm.at[:, 1 - core], v.at[:, :, cols]))
    multiply(n_g - 1, (1 - zl,))
    halves = [pl.ds(pl.multiple_of((1 - core) * 128, 128), 128), pl.ds(pl.multiple_of(core * 128, 128), 128)]
    parts = [remote(rot.at[1 - zl, half], rot_in.at[half], over, new(), new()) for half in halves]
    at_end.extend(p.wait_send for p in parts)
    multiply(n_g - 1, (zl,))

    def square(i):
        parts[i].wait_recv()
        value = rot[zl, halves[i], :] + rot_in[halves[i], :]
        return value * value

    sq[...] = square(0)
    last = swap(sq, sq_in)
    mine = square(1)
    last.wait_recv()
    out_ref[...] = mine + sq_in[...]
    for finish in at_end:
        finish()
    assert used[0] == N_SEMS, used[0]


def body(out_grad, inputs, basis_out, basis_in, correction):
    tokens = out_grad.shape[0]
    half = tokens // GROUPS
    sizes = [[n for _, n in c] for c in CHUNKS]
    both = sizes[0] + sizes[1]
    scratch = [
        pltpu.VMEM((CHIPS, 256, 256), BF16),
        pltpu.VMEM((CHIPS, 256, 256), BF16),
        pltpu.VMEM((128, 256), F32),
        pltpu.VMEM((128, 256), F32),
        pltpu.VMEM((2, 256, 256), F32),
        pltpu.VMEM((256, 256), F32),
        pltpu.SemaphoreType.DMA((N_SEMS,)),
    ]
    scratch += [pltpu.VMEM((CHIPS, GROUPS, n, 256), BF16) for n in both]
    scratch += [pltpu.VMEM((GROUPS, n, 256), F32) for n in both]
    scratch += [pltpu.VMEM((n, 256), F32) for n in both]
    scratch += [pltpu.VMEM((CHIPS, n, 256), BF16) for n in sizes[0]]
    scratch += [pltpu.VMEM((n, 256), BF16) for n in sizes[1]]
    scratch += [pltpu.VMEM((2, 8, half, 256), BF16), pltpu.VMEM((8, half, 256), BF16)]
    squares = pl.pallas_call(
        kernel,
        name="ekfac",
        out_shape=jax.ShapeDtypeStruct(correction.shape, F32),
        in_specs=[pl.BlockSpec(memory_space=pl.ANY)] * 4,
        out_specs=pl.BlockSpec(memory_space=pltpu.VMEM),
        scratch_shapes=scratch,
        compiler_params=pltpu.CompilerParams(collective_id=0, has_side_effects=True, vmem_limit_bytes=62 << 20),
        cost_estimate=pl.CostEstimate(flops=3 * 10**9, bytes_accessed=5 * 10**6, transcendentals=0),
    )(
        out_grad.reshape(GROUPS, half, 256),
        inputs.reshape(GROUPS, half, 256),
        basis_out.reshape(CHIPS, 2, 256, 128),
        basis_in.reshape(CHIPS, 2, 256, 128),
    )
    return correction + squares / (tokens * lax.axis_size("ctx"))


def solution(mesh):
    return jax.shard_map(
        body,
        mesh=mesh,
        in_specs=(P("ctx", "basis"), P("ctx", "basis"), P(None, "basis"), P(None, "basis"), P("basis", "ctx")),
        out_specs=P("basis", "ctx"),
        check_vma=False,
    )
```

```python
import jax
import jax.numpy as jnp
from jax import lax
from jax.experimental import pallas as pl
from jax.experimental.pallas import tpu as pltpu
from jax.sharding import PartitionSpec as P

MESH = pl.DeviceIdType.MESH
GROUPS = 2
CHIPS = 16
CHUNKS = (((0, 80), (80, 64)), ((0, 80), (80, 64)))
ORDER = (
    "x0", "x1", "x0", "x1", "b0", "x0", "x1", "x0", "x1", "x0", "x1", "x2", "x3", "x0", "r0", "x1",
    "r1", "s0", "m0", "m0", "s1", "m1", "m1", "x2", "x3", "m0", "m1", "m0", "m1", "m0", "m1", "x2",
    "x3", "x2", "x3", "m0", "m1", "x2", "x3", "x2", "r2", "x3", "s2", "g0", "r3", "g0", "s3", "g1",
    "g0", "g0", "m0", "m1", "g0", "f0", "g1",
)
N_SEMS = 85
F32 = jnp.float32
BF16 = jnp.bfloat16


def kernel(grad_hbm, in_hbm, bo_hbm, bi_hbm, out_ref, *scratch):
    n_a, n_g = (len(c) for c in CHUNKS)
    n_q = n_a + n_g
    pieces = CHUNKS[0] + CHUNKS[1]
    (bo_v, bi_v, sq, sq_in, rot, rot_in, sems), rest = scratch[:7], scratch[7:]
    x_land, part, part_in = rest[:n_q], rest[n_q:2 * n_q], rest[2 * n_q:3 * n_q]
    a_ga, g_mine, a_all, g_all = rest[3 * n_q:3 * n_q + n_a], rest[3 * n_q + n_a:4 * n_q], rest[4 * n_q], rest[4 * n_q + 1]

    ctx = lax.axis_index("ctx")
    basis = lax.axis_index("basis")
    y, zl = lax.rem(ctx, 8), lax.div(ctx, 8)
    core = lax.rem(basis, 2)
    chip = lax.div(basis, 2)
    x, zh = lax.rem(chip, 4), lax.div(chip, 4)

    def wrap(v, n):
        return lax.rem(v + n, n)

    def chip_of(dz, dx):
        return wrap(zh - dz, 4) * 4 + wrap(x - dx, 4)

    def at_chip(p, k):
        return {"ctx": ctx, "basis": p * 2 + k}

    def at_ctx(c):
        return {"ctx": c, "basis": basis}

    def ctx_of(dy, dz):
        return wrap(zl - dz, 2) * 8 + wrap(y - dy, 8)

    sibling = at_chip(chip, 1 - core)
    x_up, x_dn = at_chip(chip_of(0, -1), core), at_chip(chip_of(0, 1), core)
    z_up, z_dn = at_chip(chip_of(-1, 0), core), at_chip(chip_of(1, 0), core)
    peers = [at_ctx(ctx_of(-r, 0)) for r in range(1, 8)]
    over = at_ctx(ctx_of(0, 1))

    barrier = pltpu.get_barrier_semaphore()
    others = [sibling, over, x_up, x_dn, z_up, z_dn] + peers
    for other in others:
        pl.semaphore_signal(barrier, inc=1, device_id=other, device_id_type=MESH)

    used = [0]
    at_end = []

    def new():
        used[0] += 1
        return sems.at[used[0] - 1]

    def take(sem, ref):
        pltpu.make_async_copy(ref, ref, sem).wait()

    def local(src, dst):
        copy = pltpu.make_async_copy(src, dst, new())
        copy.start()
        return copy

    def remote(src, dst, device, send, recv):
        copy = pltpu.make_async_remote_copy(
            src_ref=src, dst_ref=dst, send_sem=send, recv_sem=recv, device_id=device, device_id_type=MESH
        )
        copy.start()
        return copy

    def swap(src, dst):
        copy = remote(src, dst, sibling, new(), new())
        at_end.append(copy.wait_send)
        return copy

    cols = pl.ds(pl.multiple_of(core * 128, 128), 128)
    b_copies = [[local(hbm.at[:, core], v.at[:, :, cols])] for hbm, v in ((bi_hbm, bi_v), (bo_hbm, bo_v))]
    shards, own_copies = [], []
    for q in range(n_q):
        shards.append((in_hbm if q < n_a else grad_hbm).at[:, pl.ds(*pieces[q])])
        own_copies.append(local(shards[q], x_land[q].at[chip]))

    pl.semaphore_wait(barrier, len(others))

    def gather(own, land, odd, got=lambda dz, dx: None):
        send, z1, z2, x2 = (new() for _ in range(4))
        x1 = {dz: new() for dz in (0, 1, -1, 2)}

        def slot(dz, dx):
            return land.at[chip_of(dz, dx)]

        def hop(dz, dx, device, recv, src=None, part=None):
            dst = slot(dz, dx)
            if part is not None:
                dst = dst.at[part]
            remote(dst if src is None else src, dst, device, send, recv)

        hop(0, 0, z_up, z1, own)
        hop(0, 0, z_dn, z1, own)
        yield
        hop(0, 0, x_up, x1[0], own)
        hop(0, 0, x_dn, x1[0], own)
        got(0, 0)
        yield
        take(z1, land.at[pl.ds(0, 2)])
        if land.ndim == 4:
            hop(1, 0, z_up, z2, part=0)
            hop(-1, 0, z_dn, z2, part=1)
        elif odd:
            hop(-1, 0, z_dn, z2)
        else:
            hop(1, 0, z_up, z2)
        for dz in (1, -1):
            hop(dz, 0, x_up, x1[dz])
            hop(dz, 0, x_dn, x1[dz])
        got(1, 0)
        got(-1, 0)
        yield
        take(z2, land.at[0])
        hop(2, 0, x_up, x1[2])
        hop(2, 0, x_dn, x1[2])
        got(2, 0)
        yield
        for i, dz in enumerate((0, 1, -1, 2)):
            take(x1[dz], land.at[pl.ds(0, 2)])
            if i % 2:
                hop(dz, -1, x_dn, x2)
            else:
                hop(dz, 1, x_up, x2)
            got(dz, 1)
            got(dz, -1)
        yield
        take(x2, land.at[pl.ds(0, 4)])
        for dz in (0, 1, -1, 2):
            got(dz, 2)
        at_end.append(lambda: take(send, land.at[pl.ds(0, 15)]))
        yield

    def spread_a(j):
        send, recv, kept = new(), new(), new()

        def got(dz, dx):
            owner = chip_of(dz, dx)
            target = lax.rem(owner, 8)
            src, dst = a_ga[j].at[owner], a_all.at[lax.div(owner, 8), y, pl.ds(*CHUNKS[0][j])]

            @pl.when(target != y)
            def _():
                remote(src, dst, at_ctx(zl * 8 + target), send, recv)

            @pl.when(target == y)
            def _():
                pltpu.make_async_copy(src, dst, kept).start()

        yield from gather(a_ga[j].at[chip], a_ga[j], j % 2 == 1, got)
        take(recv, a_ga[j].at[pl.ds(0, 14)])
        take(kept, a_ga[j].at[pl.ds(0, 2)])
        at_end.append(lambda: take(send, a_ga[j].at[pl.ds(0, 14)]))
        yield

    def spread_g(j):
        rows = pl.ds(*CHUNKS[1][j])
        here = g_all.at[y, rows]
        send = new()
        if j + 1 < n_g:
            hops = [new() for _ in range(4)]
            up, dn = peers[0], peers[6]

            def hop(i):
                above, below = (g_all.at[lax.rem(y + 8 + d, 8), rows] for d in (-i, i))
                if i < 4:
                    remote(above if i else g_mine[j], above, up, send, hops[i])
                if i < 3:
                    remote(below if i else g_mine[j], below, dn, send, hops[i])

            hop(0)
            yield
            for i in range(1, 4):
                take(hops[i - 1], g_all.at[pl.ds(0, 2), rows])
                hop(i)
                yield
            take(hops[3], g_all.at[0, rows])
        else:
            recv = new()
            for peer in peers:
                remote(g_mine[j], here, peer, send, recv)
            yield
            take(recv, g_all.at[pl.ds(0, 7), rows])
        at_end.append(lambda: take(send, g_all.at[pl.ds(0, 7), rows]))
        yield

    swaps = {}

    def rotate(q):
        i = 0 if q < n_a else 1
        v = (bi_v, bo_v)[i]
        if q in (0, n_a):
            own, other = b_copies[i]
            own.wait()
            other.wait_recv()
        own_copies[q].wait()
        n = pieces[q][1]

        def add(i, total):
            for s in range(4):
                s += 4 * i
                total += jnp.dot(x_land[q][s].reshape(2 * n, 256), v[s], preferred_element_type=F32)
            return total

        total = lax.fori_loop(0, CHIPS // 4, add, jnp.zeros((2 * n, 256), F32))
        part[q][...] = total.reshape(2, n, 256)
        swaps[q] = swap(part[q].at[1 - core], part_in[q])

    def settle(q):
        swaps[q].wait_recv()
        value = (part[q][core] + part_in[q][...]).astype(BF16)
        if q < n_a:
            a_ga[q][chip] = value
            gens["m", q] = spread_a(q)
        else:
            j = q - n_a
            g_mine[j][...] = value
            g_all[y, pl.ds(*pieces[q]), :] = value
            gens["g", j] = spread_g(j)

    def multiply(j, tiles):
        first, n = CHUNKS[1][j]
        rows = pl.ds(first, n)

        def add(i, _):
            some = pl.ds(i * 4, 4)
            left = g_all[some, rows, :].reshape(4 * n, 256)
            for h in tiles:
                right = a_all[h, some, rows, :].reshape(4 * n, 256)
                rot[h] += lax.dot_general(left, right, (((0,), (0,)), ((), ())), preferred_element_type=F32)
            return 0

        lax.fori_loop(0, 2, add, 0)

    gens = {("x", q): gather(shards[q], x_land[q], q % 2 == 1) for q in range(n_q)}
    rot[...] = jnp.zeros((2, 256, 256), F32)
    for step in ORDER:
        op, q = step[0], int(step[1])
        if op in "xmg":
            next(gens[op, q])
        elif op == "r":
            rotate(q)
        elif op == "s":
            settle(q)
        elif op == "f":
            multiply(q, (0, 1))
        else:
            for copies, hbm, v in ((b_copies[0], bi_hbm, bi_v), (b_copies[1], bo_hbm, bo_v)):
                copies.append(swap(hbm.at[:, 1 - core], v.at[:, :, cols]))
    multiply(n_g - 1, (1 - zl,))
    halves = [pl.ds(pl.multiple_of((1 - core) * 128, 128), 128), pl.ds(pl.multiple_of(core * 128, 128), 128)]
    parts = [remote(rot.at[1 - zl, half], rot_in.at[half], over, new(), new()) for half in halves]
    at_end.extend(p.wait_send for p in parts)
    multiply(n_g - 1, (zl,))

    def square(i):
        parts[i].wait_recv()
        value = rot[zl, halves[i], :] + rot_in[halves[i], :]
        return value * value

    sq[...] = square(0)
    last = swap(sq, sq_in)
    mine = square(1)
    last.wait_recv()
    out_ref[...] = mine + sq_in[...]
    for finish in at_end:
        finish()
    assert used[0] == N_SEMS, used[0]


def body(out_grad, inputs, basis_out, basis_in, correction):
    tokens = out_grad.shape[0]
    half = tokens // GROUPS
    sizes = [[n for _, n in c] for c in CHUNKS]
    both = sizes[0] + sizes[1]
    scratch = [
        pltpu.VMEM((CHIPS, 256, 256), BF16),
        pltpu.VMEM((CHIPS, 256, 256), BF16),
        pltpu.VMEM((128, 256), F32),
        pltpu.VMEM((128, 256), F32),
        pltpu.VMEM((2, 256, 256), F32),
        pltpu.VMEM((256, 256), F32),
        pltpu.SemaphoreType.DMA((N_SEMS,)),
    ]
    scratch += [pltpu.VMEM((CHIPS, GROUPS, n, 256), BF16) for n in both]
    scratch += [pltpu.VMEM((GROUPS, n, 256), F32) for n in both]
    scratch += [pltpu.VMEM((n, 256), F32) for n in both]
    scratch += [pltpu.VMEM((CHIPS, n, 256), BF16) for n in sizes[0]]
    scratch += [pltpu.VMEM((n, 256), BF16) for n in sizes[1]]
    scratch += [pltpu.VMEM((2, 8, half, 256), BF16), pltpu.VMEM((8, half, 256), BF16)]
    squares = pl.pallas_call(
        kernel,
        name="ekfac",
        out_shape=jax.ShapeDtypeStruct(correction.shape, F32),
        in_specs=[pl.BlockSpec(memory_space=pl.ANY)] * 4,
        out_specs=pl.BlockSpec(memory_space=pltpu.VMEM),
        scratch_shapes=scratch,
        compiler_params=pltpu.CompilerParams(collective_id=0, has_side_effects=True, vmem_limit_bytes=62 << 20),
        cost_estimate=pl.CostEstimate(flops=3 * 10**9, bytes_accessed=5 * 10**6, transcendentals=0),
    )(
        out_grad.reshape(GROUPS, half, 256),
        inputs.reshape(GROUPS, half, 256),
        basis_out.reshape(CHIPS, 2, 256, 128),
        basis_in.reshape(CHIPS, 2, 256, 128),
    )
    return correction + squares / (tokens * lax.axis_size("ctx"))


def solution(mesh):
    return jax.shard_map(
        body,
        mesh=mesh,
        in_specs=(P("ctx", "basis"), P("ctx", "basis"), P(None, "basis"), P(None, "basis"), P("basis", "ctx")),
        out_specs=P("basis", "ctx"),
        check_vma=False,
    )
```

```python
import jax
import jax.numpy as jnp
from jax import lax
from jax.experimental import pallas as pl
from jax.experimental.pallas import tpu as pltpu
from jax.sharding import PartitionSpec as P

MESH = pl.DeviceIdType.MESH
GROUPS = 2
CHIPS = 16
CHUNKS = (((0, 80), (80, 64)), ((0, 80), (80, 64)))
ORDER = (
    "x0", "x1", "x0", "x1", "b0", "x0", "x1", "x0", "x1", "x0", "x1", "x2", "x3", "x0", "r0", "x1",
    "r1", "s0", "m0", "m0", "s1", "m1", "m1", "x2", "x3", "m0", "m1", "m0", "m1", "m0", "m1", "x2",
    "x3", "x2", "x3", "m0", "m1", "x2", "x3", "x2", "r2", "s2", "g0", "x3", "r3", "g0", "s3", "g1",
    "g0", "g0", "m0", "m1", "g0", "f0", "g1",
)
N_SEMS = 85
F32 = jnp.float32
BF16 = jnp.bfloat16


def kernel(grad_hbm, in_hbm, bo_hbm, bi_hbm, out_ref, *scratch):
    n_a, n_g = (len(c) for c in CHUNKS)
    n_q = n_a + n_g
    pieces = CHUNKS[0] + CHUNKS[1]
    (bo_v, bi_v, sq, sq_in, rot, rot_in, sems), rest = scratch[:7], scratch[7:]
    x_land, part, part_in = rest[:n_q], rest[n_q:2 * n_q], rest[2 * n_q:3 * n_q]
    a_ga, g_mine, a_all, g_all = rest[3 * n_q:3 * n_q + n_a], rest[3 * n_q + n_a:4 * n_q], rest[4 * n_q], rest[4 * n_q + 1]

    ctx = lax.axis_index("ctx")
    basis = lax.axis_index("basis")
    y, zl = lax.rem(ctx, 8), lax.div(ctx, 8)
    core = lax.rem(basis, 2)
    chip = lax.div(basis, 2)
    x, zh = lax.rem(chip, 4), lax.div(chip, 4)

    def wrap(v, n):
        return lax.rem(v + n, n)

    def chip_of(dz, dx):
        return wrap(zh - dz, 4) * 4 + wrap(x - dx, 4)

    def at_chip(p, k):
        return {"ctx": ctx, "basis": p * 2 + k}

    def at_ctx(c):
        return {"ctx": c, "basis": basis}

    def ctx_of(dy, dz):
        return wrap(zl - dz, 2) * 8 + wrap(y - dy, 8)

    sibling = at_chip(chip, 1 - core)
    x_up, x_dn = at_chip(chip_of(0, -1), core), at_chip(chip_of(0, 1), core)
    z_up, z_dn = at_chip(chip_of(-1, 0), core), at_chip(chip_of(1, 0), core)
    peers = [at_ctx(ctx_of(-r, 0)) for r in range(1, 8)]
    over = at_ctx(ctx_of(0, 1))

    barrier = pltpu.get_barrier_semaphore()
    others = [sibling, over, x_up, x_dn, z_up, z_dn] + peers
    for other in others:
        pl.semaphore_signal(barrier, inc=1, device_id=other, device_id_type=MESH)

    used = [0]
    at_end = []

    def new():
        used[0] += 1
        return sems.at[used[0] - 1]

    def take(sem, ref):
        pltpu.make_async_copy(ref, ref, sem).wait()

    def local(src, dst):
        copy = pltpu.make_async_copy(src, dst, new())
        copy.start()
        return copy

    def remote(src, dst, device, send, recv):
        copy = pltpu.make_async_remote_copy(
            src_ref=src, dst_ref=dst, send_sem=send, recv_sem=recv, device_id=device, device_id_type=MESH
        )
        copy.start()
        return copy

    def swap(src, dst):
        copy = remote(src, dst, sibling, new(), new())
        at_end.append(copy.wait_send)
        return copy

    cols = pl.ds(pl.multiple_of(core * 128, 128), 128)
    b_copies = [[local(hbm.at[:, core], v.at[:, :, cols])] for hbm, v in ((bi_hbm, bi_v), (bo_hbm, bo_v))]
    shards, own_copies = [], []
    for q in range(n_q):
        shards.append((in_hbm if q < n_a else grad_hbm).at[:, pl.ds(*pieces[q])])
        own_copies.append(local(shards[q], x_land[q].at[chip]))

    pl.semaphore_wait(barrier, len(others))

    def gather(own, land, odd, got=lambda dz, dx: None):
        send, z1, z2, x2 = (new() for _ in range(4))
        x1 = {dz: new() for dz in (0, 1, -1, 2)}

        def slot(dz, dx):
            return land.at[chip_of(dz, dx)]

        def hop(dz, dx, device, recv, src=None, part=None):
            dst = slot(dz, dx)
            if part is not None:
                dst = dst.at[part]
            remote(dst if src is None else src, dst, device, send, recv)

        hop(0, 0, z_up, z1, own)
        hop(0, 0, z_dn, z1, own)
        yield
        hop(0, 0, x_up, x1[0], own)
        hop(0, 0, x_dn, x1[0], own)
        got(0, 0)
        yield
        take(z1, land.at[pl.ds(0, 2)])
        if land.ndim == 4:
            hop(1, 0, z_up, z2, part=0)
            hop(-1, 0, z_dn, z2, part=1)
        elif odd:
            hop(-1, 0, z_dn, z2)
        else:
            hop(1, 0, z_up, z2)
        for dz in (1, -1):
            hop(dz, 0, x_up, x1[dz])
            hop(dz, 0, x_dn, x1[dz])
        got(1, 0)
        got(-1, 0)
        yield
        take(z2, land.at[0])
        hop(2, 0, x_up, x1[2])
        hop(2, 0, x_dn, x1[2])
        got(2, 0)
        yield
        for i, dz in enumerate((0, 1, -1, 2)):
            take(x1[dz], land.at[pl.ds(0, 2)])
            if i % 2:
                hop(dz, -1, x_dn, x2)
            else:
                hop(dz, 1, x_up, x2)
            got(dz, 1)
            got(dz, -1)
        yield
        take(x2, land.at[pl.ds(0, 4)])
        for dz in (0, 1, -1, 2):
            got(dz, 2)
        at_end.append(lambda: take(send, land.at[pl.ds(0, 15)]))
        yield

    def spread_a(j):
        send, recv, kept = new(), new(), new()

        def got(dz, dx):
            owner = chip_of(dz, dx)
            target = lax.rem(owner, 8)
            src, dst = a_ga[j].at[owner], a_all.at[lax.div(owner, 8), y, pl.ds(*CHUNKS[0][j])]

            @pl.when(target != y)
            def _():
                remote(src, dst, at_ctx(zl * 8 + target), send, recv)

            @pl.when(target == y)
            def _():
                pltpu.make_async_copy(src, dst, kept).start()

        yield from gather(a_ga[j].at[chip], a_ga[j], j % 2 == 1, got)
        take(recv, a_ga[j].at[pl.ds(0, 14)])
        take(kept, a_ga[j].at[pl.ds(0, 2)])
        at_end.append(lambda: take(send, a_ga[j].at[pl.ds(0, 14)]))
        yield

    def spread_g(j):
        rows = pl.ds(*CHUNKS[1][j])
        here = g_all.at[y, rows]
        send = new()
        if j + 1 < n_g:
            hops = [new() for _ in range(4)]
            up, dn = peers[0], peers[6]

            def hop(i):
                above, below = (g_all.at[lax.rem(y + 8 + d, 8), rows] for d in (-i, i))
                if i < 4:
                    remote(above if i else g_mine[j], above, up, send, hops[i])
                if i < 3:
                    remote(below if i else g_mine[j], below, dn, send, hops[i])

            hop(0)
            yield
            for i in range(1, 4):
                take(hops[i - 1], g_all.at[pl.ds(0, 2), rows])
                hop(i)
                yield
            take(hops[3], g_all.at[0, rows])
        else:
            recv = new()
            for i in (3, 2, 4, 1, 5, 0, 6):
                remote(g_mine[j], here, peers[i], send, recv)
            yield
            take(recv, g_all.at[pl.ds(0, 7), rows])
        at_end.append(lambda: take(send, g_all.at[pl.ds(0, 7), rows]))
        yield

    swaps = {}

    def rotate(q):
        i = 0 if q < n_a else 1
        v = (bi_v, bo_v)[i]
        if q in (0, n_a):
            own, other = b_copies[i]
            own.wait()
            other.wait_recv()
        own_copies[q].wait()
        n = pieces[q][1]

        def add(i, total):
            for s in range(4):
                s += 4 * i
                total += jnp.dot(x_land[q][s].reshape(2 * n, 256), v[s], preferred_element_type=F32)
            return total

        total = lax.fori_loop(0, CHIPS // 4, add, jnp.zeros((2 * n, 256), F32))
        part[q][...] = total.reshape(2, n, 256)
        swaps[q] = swap(part[q].at[1 - core], part_in[q])

    def settle(q):
        swaps[q].wait_recv()
        value = (part[q][core] + part_in[q][...]).astype(BF16)
        if q < n_a:
            a_ga[q][chip] = value
            gens["m", q] = spread_a(q)
        else:
            j = q - n_a
            g_mine[j][...] = value
            g_all[y, pl.ds(*pieces[q]), :] = value
            gens["g", j] = spread_g(j)

    def multiply(j, tiles):
        first, n = CHUNKS[1][j]
        rows = pl.ds(first, n)

        def add(i, _):
            some = pl.ds(i * 4, 4)
            left = g_all[some, rows, :].reshape(4 * n, 256)
            for h in tiles:
                right = a_all[h, some, rows, :].reshape(4 * n, 256)
                rot[h] += lax.dot_general(left, right, (((0,), (0,)), ((), ())), preferred_element_type=F32)
            return 0

        lax.fori_loop(0, 2, add, 0)

    gens = {("x", q): gather(shards[q], x_land[q], q % 2 == 1) for q in range(n_q)}
    rot[...] = jnp.zeros((2, 256, 256), F32)
    for step in ORDER:
        op, q = step[0], int(step[1])
        if op in "xmg":
            next(gens[op, q])
        elif op == "r":
            rotate(q)
        elif op == "s":
            settle(q)
        elif op == "f":
            multiply(q, (0, 1))
        else:
            for copies, hbm, v in ((b_copies[0], bi_hbm, bi_v), (b_copies[1], bo_hbm, bo_v)):
                copies.append(swap(hbm.at[:, 1 - core], v.at[:, :, cols]))
    multiply(n_g - 1, (1 - zl,))
    halves = [pl.ds(pl.multiple_of((1 - core) * 128, 128), 128), pl.ds(pl.multiple_of(core * 128, 128), 128)]
    parts = [remote(rot.at[1 - zl, half], rot_in.at[half], over, new(), new()) for half in halves]
    at_end.extend(p.wait_send for p in parts)
    multiply(n_g - 1, (zl,))

    def square(i):
        parts[i].wait_recv()
        value = rot[zl, halves[i], :] + rot_in[halves[i], :]
        return value * value

    sq[...] = square(0)
    last = swap(sq, sq_in)
    mine = square(1)
    last.wait_recv()
    out_ref[...] = mine + sq_in[...]
    for finish in at_end:
        finish()
    assert used[0] == N_SEMS, used[0]


def body(out_grad, inputs, basis_out, basis_in, correction):
    tokens = out_grad.shape[0]
    half = tokens // GROUPS
    sizes = [[n for _, n in c] for c in CHUNKS]
    both = sizes[0] + sizes[1]
    scratch = [
        pltpu.VMEM((CHIPS, 256, 256), BF16),
        pltpu.VMEM((CHIPS, 256, 256), BF16),
        pltpu.VMEM((128, 256), F32),
        pltpu.VMEM((128, 256), F32),
        pltpu.VMEM((2, 256, 256), F32),
        pltpu.VMEM((256, 256), F32),
        pltpu.SemaphoreType.DMA((N_SEMS,)),
    ]
    scratch += [pltpu.VMEM((CHIPS, GROUPS, n, 256), BF16) for n in both]
    scratch += [pltpu.VMEM((GROUPS, n, 256), F32) for n in both]
    scratch += [pltpu.VMEM((n, 256), F32) for n in both]
    scratch += [pltpu.VMEM((CHIPS, n, 256), BF16) for n in sizes[0]]
    scratch += [pltpu.VMEM((n, 256), BF16) for n in sizes[1]]
    scratch += [pltpu.VMEM((2, 8, half, 256), BF16), pltpu.VMEM((8, half, 256), BF16)]
    squares = pl.pallas_call(
        kernel,
        name="ekfac",
        out_shape=jax.ShapeDtypeStruct(correction.shape, F32),
        in_specs=[pl.BlockSpec(memory_space=pl.ANY)] * 4,
        out_specs=pl.BlockSpec(memory_space=pltpu.VMEM),
        scratch_shapes=scratch,
        compiler_params=pltpu.CompilerParams(collective_id=0, has_side_effects=True, vmem_limit_bytes=62 << 20),
        cost_estimate=pl.CostEstimate(flops=3 * 10**9, bytes_accessed=5 * 10**6, transcendentals=0),
    )(
        out_grad.reshape(GROUPS, half, 256),
        inputs.reshape(GROUPS, half, 256),
        basis_out.reshape(CHIPS, 2, 256, 128),
        basis_in.reshape(CHIPS, 2, 256, 128),
    )
    return correction + squares / (tokens * lax.axis_size("ctx"))


def solution(mesh):
    return jax.shard_map(
        body,
        mesh=mesh,
        in_specs=(P("ctx", "basis"), P("ctx", "basis"), P(None, "basis"), P(None, "basis"), P("basis", "ctx")),
        out_specs=P("basis", "ctx"),
        check_vma=False,
    )
```
